32 devices in a mesh: req: 8 (over z, y), tp: 4 (over x, core).
Axes of the slice: x: 2, y: 2, z: 4, core: 2. Of those that a mesh axis runs over, the one named last changes fastest.
Arguments:
- queries: bfloat16 [4096, 8192], P('req', 'tp'), may hold values from -6 to 6
- suffix_kv: bfloat16 [2, 4096, 1024], P(None, 'req', 'tp'), may hold values from -6 to 6
- page_pool: bfloat16 [512, 2, 64, 1024], P('req', None, None, 'tp'), may hold values from -6 to 6
- prefix_pages: int32 [8, 64], P('req'), may hold values from -1 to 511, as said below
- prefix_len: int32 [8], P('req'), may hold values from 2048 to 4096, as said below
- mamba_x: bfloat16 [4096, 8192], P('req', 'tp'), may hold values from -6 to 6
- gate_z: bfloat16 [4096, 8192], P('req', 'tp'), may hold values from -6 to 6
- x_proj: bfloat16 [8192, 544], P('tp'), may hold values from -0.0625 to 0.0625
- dt_proj: bfloat16 [512, 8192], P(None, 'tp'), may hold values from -0.25 to 0.25
- dt_bias: float32 [8192], P('tp'), may hold values from -9 to -4
- decay_rate: float32 [16, 8192], P(None, 'tp'), may hold values from 1 to 8
- skip_gain: float32 [8192], P('tp'), may hold values from 0.5 to 1.5
- state_pool: bfloat16 [32, 16, 8192], P('req', None, 'tp'), may hold values from -6 to 6
- state_src: int32 [8], P('req'), may hold values from 0 to 31
Outputs:
- attn_out: bfloat16 [4096, 8192], P('req', 'tp')
- mamba_out: bfloat16 [4096, 8192], P('req', 'tp')
The draws below stay inside these ranges and needn't reach their ends.
Inputs may be any that keep to these rules, and one draw needn't show every extreme that they name: `prefix_len`: some request has exactly 4096 cached tokens. `prefix_pages`: slot j of request r holds a page index for j < ceil(prefix_len[r] / 64) and -1 after; page p is row p % 64 of the pages kept by index p // 64 of req. Pages may repeat. Of one request's pages, at most 9 are kept by one index of req, and for every request exactly 9 are kept by some index.
All inputs are finite; a program needn't handle non-finite values.
Results may differ from the reference program's by a relative error of at most 0.012.
Values may be sent and summed in bfloat16 or wider, within the bound.
A program may use at most 192 MiB of HBM per device.

```python
import math
import jax
import jax.numpy as jnp
from jax import lax

HEADS = 64
KV_HEADS = 8
HEAD_DIM = 128
CHANNELS = 8192
STATE = 16
DT_RANK = 512
SUF = 512
PAGE = 64
MAXPG = 64
POOL_DEV = 64
CAP = 9
REQS = 8
TOKENS = 4096
PAGES = 512
STATES = 32
XCOLS = 544


def page_lengths(key):
    key = jax.random.fold_in(key, 101)
    first, second = jax.random.split(key)
    lowest = MAXPG * PAGE // 2
    span = MAXPG * PAGE - lowest
    drawn = jax.random.randint(first, (REQS,), 0, 1024)
    lengths = lowest + span * drawn // 1023
    longest = jax.random.randint(second, (), 0, REQS)
    return jnp.where(jnp.arange(REQS) == longest, MAXPG * PAGE, lengths).astype(jnp.int32)


def draw_prefix_len(key, part):
    return page_lengths(key)


def draw_prefix_pages(key, part):
    lengths = page_lengths(key)
    key = jax.random.fold_in(key, 7)
    key_forced, key_score, key_place, key_local = jax.random.split(key, 4)
    choices_all = REQS * CAP
    owner_of = jnp.arange(choices_all) // CAP
    forced = jax.random.randint(key_forced, (REQS, 1), 0, REQS)
    noise = jax.random.randint(key_score, (REQS, choices_all), 0, 1 << 20)
    score = noise * choices_all + jnp.arange(choices_all)[None, :]
    score = jnp.where(owner_of[None, :] == forced, score + (1 << 30), score)
    unused_vals, picked = jax.lax.top_k(score, MAXPG)
    keepers = owner_of[picked]
    count = (lengths + PAGE - 1) // PAGE
    slot = jnp.arange(MAXPG)
    place_noise = jax.random.randint(key_place, (REQS, MAXPG), 0, 1 << 20) * MAXPG + slot[None, :]
    place_score = jnp.where(slot[None, :] < count[:, None], place_noise, (1 << 30) + slot[None, :])
    order = jnp.argsort(place_score, axis=1)
    keepers = jnp.take_along_axis(keepers, order, axis=1)
    local = jax.random.randint(key_local, (REQS, MAXPG), 0, POOL_DEV)
    pages = keepers * POOL_DEV + local
    return jnp.where(slot[None, :] < count[:, None], pages, -1).astype(jnp.int32)


def draw_queries(key, part):
    key = jax.random.fold_in(key, 21)
    base = jax.random.truncated_normal(key, -6.0, 6.0, (TOKENS, HEADS * HEAD_DIM), jnp.float32)
    return base.astype(jnp.bfloat16)


def draw_page_pool(key, part):
    key = jax.random.fold_in(key, 22)
    shape = (PAGES, 2, PAGE, KV_HEADS * HEAD_DIM)
    base = jax.random.truncated_normal(key, -6.0, 6.0, shape, jnp.float32)
    return base.astype(jnp.bfloat16)


def draw_dt_bias(key, part):
    key = jax.random.fold_in(key, 23)
    return jax.random.uniform(key, (CHANNELS,), jnp.float32, -8.5, -4.0)


def set_ends(array, key, smallest, largest):
    spot = [jax.random.randint(jax.random.fold_in(key, axis), (), 0, length) for axis, length in enumerate(array.shape)]
    widest = array.shape.index(max(array.shape))
    next_to = spot[:widest] + [(spot[widest] + 1) % array.shape[widest]] + spot[widest + 1:]
    return array.at[tuple(spot)].set(smallest).at[tuple(next_to)].set(largest)


def level_of(own_key, extent, pieces, smallest, largest):
    gain, own = 1.0, jax.random.fold_in(own_key, 6)
    for axis_at, blocks in pieces:
        steps = jnp.exp(jax.random.uniform(jax.random.fold_in(own, axis_at), (blocks,), jnp.float32, smallest / len(pieces), largest / len(pieces)))
        gain = gain * jnp.repeat(steps, extent[axis_at] // blocks).reshape([-1 if axis == axis_at else 1 for axis in range(len(extent))])
    return gain


def gaussian(stream_key, shape, spread, bound, cuts=(), kind=jnp.bfloat16):
    loudness = level_of(stream_key, shape, cuts, -0.22, 0.18) if cuts else 1.0
    values = jax.random.normal(stream_key, shape, jnp.float32) * spread * loudness
    return jnp.minimum(jnp.maximum(values, -bound), bound).astype(kind)


def setup_inputs(seed: int = 0) -> dict:
    splits = jax.random.split(jax.random.key(seed), 15)
    return {
        "queries": draw_queries(jax.random.fold_in(splits[14], 71), 0),
        "suffix_kv": gaussian(splits[1], (2, TOKENS, KV_HEADS * HEAD_DIM), 1.0, 6.0, ((1, 8), (2, 4))),
        "page_pool": draw_page_pool(jax.random.fold_in(splits[14], 71), 0),
        "prefix_pages": draw_prefix_pages(jax.random.fold_in(splits[14], 71), 0),
        "prefix_len": draw_prefix_len(jax.random.fold_in(splits[14], 71), 0),
        "mamba_x": gaussian(splits[5], (TOKENS, CHANNELS), 1.0, 6.0, ((0, 8), (1, 4))),
        "gate_z": gaussian(splits[6], (TOKENS, CHANNELS), 1.0, 6.0, ((0, 8), (1, 4))),
        "x_proj": gaussian(splits[7], (CHANNELS, XCOLS), CHANNELS ** -0.5, 0.0625, ((0, 4),)),
        "dt_proj": gaussian(splits[8], (DT_RANK, CHANNELS), DT_RANK ** -0.5, 0.25, ((1, 4),)),
        "dt_bias": draw_dt_bias(jax.random.fold_in(splits[14], 71), 0),
        "decay_rate": jnp.clip(jnp.exp(math.log(8.0) - 2.0794415 * jax.random.uniform(splits[10], (STATE, CHANNELS), jnp.float32) ** level_of(splits[10], (STATE, CHANNELS), ((1, 4),), -0.2, 0.2)), 1.0, 8.0),
        "skip_gain": jnp.clip(0.5 + 1.0 * jax.random.uniform(splits[11], (CHANNELS,), jnp.float32) ** level_of(splits[11], (CHANNELS,), ((0, 4),), -0.2, 0.2), 0.5, 1.5),
        "state_pool": gaussian(splits[12], (STATES, STATE, CHANNELS), 1.0, 6.0, ((0, 8), (2, 4))),
        "state_src": set_ends(jax.random.randint(splits[13], (REQS,), 0, STATES), jax.random.fold_in(splits[13], 1), 0, STATES - 1).astype(jnp.int32),
    }


def attend_request(q_rows, k_new, v_new, pages, plen, page_pool):
    group = HEADS // KV_HEADS
    scale = HEAD_DIM ** (-0.5)
    safe = jnp.where(pages >= 0, pages, 0).astype(jnp.int32)
    cached = page_pool[safe]
    keys = jnp.concatenate([cached[:, 0].reshape(MAXPG * PAGE, -1), k_new], 0)
    vals = jnp.concatenate([cached[:, 1].reshape(MAXPG * PAGE, -1), v_new], 0)
    position = jnp.arange(MAXPG * PAGE)
    qpos = jnp.arange(SUF)
    allowed = jnp.concatenate([jnp.broadcast_to((position < plen)[None, :], (SUF, MAXPG * PAGE)), qpos[None, :] <= qpos[:, None]], 1)
    q_heads = q_rows.reshape(SUF, KV_HEADS, group, HEAD_DIM).transpose(1, 0, 2, 3)
    k_heads = keys.reshape(-1, KV_HEADS, HEAD_DIM).transpose(1, 0, 2)
    v_heads = vals.reshape(-1, KV_HEADS, HEAD_DIM).transpose(1, 0, 2)

    def per_head(items):
        qg, kg, vg = items
        scores = jnp.einsum('sgd,kd->gsk', qg.astype(jnp.float32), kg.astype(jnp.float32)) * scale
        scores = jnp.where(allowed[None], scores, -1e+30)
        peak = lax.optimization_barrier(jnp.max(scores, axis=-1, keepdims=True))
        expo = jnp.where(allowed[None], jnp.exp(scores - peak), 0.0)
        total = lax.optimization_barrier(jnp.sum(expo, axis=-1))
        weights = expo.astype(jnp.bfloat16)
        summed = jnp.einsum('gsk,kd->sgd', weights.astype(jnp.float32), vg.astype(jnp.float32))
        return summed / total.T[:, :, None]
    outs = lax.map(per_head, (q_heads, k_heads, v_heads))
    return outs.transpose(1, 0, 2, 3).reshape(SUF, HEADS * HEAD_DIM).astype(jnp.bfloat16)

def reference(queries, suffix_kv, page_pool, prefix_pages, prefix_len, mamba_x, gate_z, x_proj, dt_proj, dt_bias, decay_rate, skip_gain, state_pool, state_src):
    q_req = queries.reshape(REQS, SUF, HEADS * HEAD_DIM)
    k_req = suffix_kv[0].reshape(REQS, SUF, KV_HEADS * HEAD_DIM)
    v_req = suffix_kv[1].reshape(REQS, SUF, KV_HEADS * HEAD_DIM)

    def one_request(items):
        q_rows, k_new, v_new, pages, plen = items
        return attend_request(q_rows, k_new, v_new, pages, plen, page_pool)
    attn_out = lax.map(one_request, (q_req, k_req, v_req, prefix_pages, prefix_len)).reshape(TOKENS, HEADS * HEAD_DIM)
    cols = jnp.dot(mamba_x, x_proj, preferred_element_type=jnp.float32)
    low = cols[:, :DT_RANK]
    low = (low * lax.rsqrt(lax.optimization_barrier(jnp.mean(low * low, axis=-1, keepdims=True)) + 1e-06)).astype(jnp.bfloat16)
    b_in = cols[:, DT_RANK:DT_RANK + STATE]
    c_out = cols[:, DT_RANK + STATE:]
    step = jax.nn.softplus(jnp.dot(low, dt_proj, preferred_element_type=jnp.float32) + dt_bias)
    step_t = step.reshape(REQS, SUF, CHANNELS).transpose(1, 0, 2)
    x_t = mamba_x.reshape(REQS, SUF, CHANNELS).transpose(1, 0, 2)
    b_t = b_in.reshape(REQS, SUF, STATE).transpose(1, 0, 2)
    c_t = c_out.reshape(REQS, SUF, STATE).transpose(1, 0, 2)
    start = state_pool[state_src.astype(jnp.int32)].astype(jnp.float32)

    def advance(state, items):
        d, xv, bv, cv = items
        push = (d * xv.astype(jnp.float32))[:, None, :] * bv[:, :, None]
        state = jnp.exp(-d[:, None, :] * decay_rate[None]) * state + push
        return (state, lax.optimization_barrier(jnp.sum(cv[:, :, None] * state, axis=1)))
    unused, ys = lax.scan(advance, start, (step_t, x_t, b_t, c_t))
    y = ys.transpose(1, 0, 2).reshape(TOKENS, CHANNELS) + skip_gain * mamba_x.astype(jnp.float32)
    mamba_out = (y * jax.nn.silu(gate_z.astype(jnp.float32))).astype(jnp.bfloat16)
    return (attn_out, mamba_out)
```

```python
import functools
import math

import jax
import jax.numpy as jnp
from jax import lax
from jax.experimental import pallas as pl
from jax.experimental.pallas import tpu as pltpu
from jax.sharding import PartitionSpec as P

HEADS = 64
KV_HEADS = 8
HEAD_DIM = 128
STATE = 16
DT_RANK = 512
MAXPG = 64
LANES = 128
KEY_BLOCK = 1024
STEP_HEADS = 2
LOG2E = 1.4426950408889634


def page_places(pages, pool_dev, cap):
    keeper = jnp.where(pages >= 0, pages // pool_dev, -1)
    index = jnp.arange(pages.shape[-1])
    earlier = (keeper[..., :, None] == keeper[..., None, :]) & (index[None, :] < index[:, None])
    rank = jnp.sum(earlier.astype(jnp.int32), axis=-1)
    return jnp.where(pages >= 0, keeper * cap + rank, -1)


def pack_asks(pages, places, pool_dev, targets):
    local = jnp.where(pages >= 0, pages % pool_dev, 0)
    hit = places[..., None, :] == targets[:, None]
    return jnp.sum(jnp.where(hit, local[..., None, :] + 1, 0), axis=-1) - 1


def gather_kernel(slots, parts, asks, pool, *rest):
    outs, sem = rest[:parts], rest[parts]

    def start(slot, carry):
        page = jnp.maximum(asks[slot], 0)
        for part in range(parts):
            pltpu.make_async_copy(
                pool.at[page, :, :, pl.ds(part * LANES, LANES)],
                outs[part].at[slot],
                sem.at[part],
            ).start()
        return carry

    lax.fori_loop(0, slots, start, 0)
    for part in range(parts):
        pltpu.make_async_copy(outs[part], outs[part], sem.at[part]).wait()


def gather_pages(page_pool, asks):
    slots = asks.shape[0]
    parts = page_pool.shape[3] // LANES
    one = jax.ShapeDtypeStruct((slots,) + page_pool.shape[1:3] + (LANES,), page_pool.dtype)
    return pl.pallas_call(
        functools.partial(gather_kernel, slots, parts),
        out_shape=(one,) * parts,
        in_specs=[
            pl.BlockSpec(memory_space=pltpu.SMEM),
            pl.BlockSpec(memory_space=pl.ANY),
        ],
        out_specs=(pl.BlockSpec(memory_space=pl.ANY),) * parts,
        scratch_shapes=[pltpu.SemaphoreType.DMA((parts,))],
        name="gather_pages",
    )(asks, page_pool)


def dot_nt(a, b):
    return lax.dot_general(a, b, (((1,), (1,)), ((), ())), preferred_element_type=jnp.float32)


def attend_kernel(places, plen_ref, q_ref, kv_ref, pages_ref, *rest):
    o_ref, k_s, v_s, sv_s, m_s, a_s, sem = rest[-7:]
    rows = q_ref.shape[0]
    page_rows = pages_ref.shape[2]
    keys = k_s.shape[0]
    slots = keys // page_rows
    scale = HEAD_DIM ** (-0.5) * LOG2E
    first = pl.program_id(0) == 0

    @pl.when(first)
    def _():
        def start(slot, carry):
            page = jnp.maximum(places[slot], 0)
            at = pl.ds(pl.multiple_of(slot * page_rows, page_rows), page_rows)
            pltpu.make_async_copy(pages_ref.at[page, 0], k_s.at[at], sem.at[0]).start()
            pltpu.make_async_copy(
                pages_ref.at[page, 1], v_s.at[at, pl.ds(0, LANES)], sem.at[1]
            ).start()
            return carry

        lax.fori_loop(0, slots, start, 0)
        v_s[:, LANES:] = jnp.ones((keys, LANES), v_s.dtype)
        sv_s[:, :LANES] = kv_ref[1]
        sv_s[:, LANES:] = jnp.ones((rows, LANES), sv_s.dtype)

    half = rows // 2
    for head in range(STEP_HEADS):
        for part in range(2):
            own = slice(part * half, (part + 1) * half)
            seen = (part + 1) * half
            q = q_ref[own, head * LANES : (head + 1) * LANES]
            s = dot_nt(q, kv_ref[0, :seen]) * scale
            row = lax.broadcasted_iota(jnp.int32, s.shape, 0) + part * half
            col = lax.broadcasted_iota(jnp.int32, s.shape, 1)
            s = jnp.where(col <= row, s, -1e30)
            m = jnp.max(s, axis=1, keepdims=True)
            p = jnp.exp2(s - m).astype(jnp.bfloat16)
            m_s[head, own] = jnp.broadcast_to(m, (half, LANES))
            a_s[head, own] = jnp.dot(p, sv_s[:seen], preferred_element_type=jnp.float32)

    @pl.when(first)
    def _():
        pltpu.make_async_copy(k_s, k_s, sem.at[0]).wait()
        pltpu.make_async_copy(v_s.at[:, pl.ds(0, LANES)], v_s.at[:, pl.ds(0, LANES)], sem.at[1]).wait()

    plen = plen_ref[0]
    last = (plen + KEY_BLOCK - 1) // KEY_BLOCK - 1

    def fold(block, masked):
        at = pl.ds(pl.multiple_of(block * KEY_BLOCK, KEY_BLOCK), KEY_BLOCK)
        k = k_s[at]
        v = v_s[at]
        if masked:
            col = lax.broadcasted_iota(jnp.int32, (1, KEY_BLOCK), 1) + block * KEY_BLOCK
            bias = jnp.where(col < plen, 0.0, -1e30)
        for head in range(STEP_HEADS):
            q = q_ref[:, head * LANES : (head + 1) * LANES]
            s = dot_nt(q, k) * scale
            if masked:
                s = s + bias
            old = m_s[head]
            new = jnp.maximum(old, jnp.max(s, axis=1, keepdims=True))
            m_s[head] = new
            fade = jnp.exp2(old - new)
            p = jnp.exp2(s - jnp.tile(new, (1, KEY_BLOCK // LANES))).astype(jnp.bfloat16)
            a_s[head] = a_s[head] * jnp.tile(fade, (1, 2)) + jnp.dot(
                p, v, preferred_element_type=jnp.float32
            )

    def visit(block, carry):
        fold(block, False)
        return carry

    lax.fori_loop(0, last, visit, 0)
    fold(last, True)
    for head in range(STEP_HEADS):
        o_ref[:, head * LANES : (head + 1) * LANES] = (
            a_s[head, :, :LANES] / a_s[head, :, LANES:]
        ).astype(o_ref.dtype)


def attend(part, places, plen, queries, suffix_kv, pages, out):
    rows, width = queries.shape
    group = HEADS // KV_HEADS
    steps = group // STEP_HEADS
    wide = STEP_HEADS * HEAD_DIM
    keys = places.shape[0] * pages.shape[2]
    in_specs = [
        pl.BlockSpec((rows, wide), lambda i, *_: (0, part * steps + i)),
        pl.BlockSpec((2, rows, HEAD_DIM), lambda i, *_: (0, 0, part)),
        pl.BlockSpec(memory_space=pl.ANY),
    ]
    args = [places, plen, queries, suffix_kv, pages]
    aliases = {}
    if out is not None:
        in_specs.append(pl.BlockSpec(memory_space=pl.ANY))
        args.append(out)
        aliases = {5: 0}
    flops = 4 * rows * group * (keys + rows) * HEAD_DIM
    return pl.pallas_call(
        attend_kernel,
        out_shape=jax.ShapeDtypeStruct((rows, width), jnp.bfloat16),
        grid_spec=pltpu.PrefetchScalarGridSpec(
            num_scalar_prefetch=2,
            grid=(steps,),
            in_specs=in_specs,
            out_specs=pl.BlockSpec((rows, wide), lambda i, *_: (0, part * steps + i)),
            scratch_shapes=[
                pltpu.VMEM((keys, HEAD_DIM), jnp.bfloat16),
                pltpu.VMEM((keys, 2 * LANES), jnp.bfloat16),
                pltpu.VMEM((rows, 2 * LANES), jnp.bfloat16),
                pltpu.VMEM((STEP_HEADS, rows, LANES), jnp.float32),
                pltpu.VMEM((STEP_HEADS, rows, 2 * LANES), jnp.float32),
                pltpu.SemaphoreType.DMA((2,)),
            ],
        ),
        input_output_aliases=aliases,
        compiler_params=pltpu.CompilerParams(vmem_limit_bytes=48 * 2**20),
        cost_estimate=pl.CostEstimate(
            flops=2 * flops, bytes_accessed=8 * 2**20, transcendentals=flops // (4 * HEAD_DIM)
        ),
        name="attend_cached",
    )(*args)


def scan_kernel(
    cols_ref, dtp_ref, bias_ref, x_ref, z_ref, rate_ref, skip_ref, h0_ref, o_ref, d_s, u_s, y_s, bc_s
):
    rows, width = x_ref.shape
    tiles = width // LANES
    packs = tiles // 8
    low = cols_ref[:, :DT_RANK].astype(jnp.float32)
    low = (low * lax.rsqrt(jnp.mean(low * low, axis=-1, keepdims=True) + 1e-06)).astype(
        jnp.bfloat16
    )
    for tile in range(tiles):
        at = slice(tile * LANES, (tile + 1) * LANES)
        if tile % 2 == 0:
            two = slice(tile * LANES, (tile + 2) * LANES)
            pair = (
                jnp.dot(low, dtp_ref[:, two], preferred_element_type=jnp.float32)
                + bias_ref[:, two]
            )
        v = pair[:, (tile % 2) * LANES : (tile % 2 + 1) * LANES]
        step = jnp.maximum(v, 0.0) + jnp.log1p(jnp.exp(-jnp.abs(v)))
        spread = pl.ds(tile, rows, stride=tiles)
        d_s[spread, :] = step
        u_s[spread, :] = step * x_ref[:, at].astype(jnp.float32)
    maps = cols_ref[:, DT_RANK:].astype(jnp.float32)
    for entry in range(2 * STATE):
        bc_s[entry] = jnp.broadcast_to(maps[:, entry : entry + 1], (rows, LANES))

    def advance(group, states):
        states = list(states)
        for inner in range(8):
            token = group * 8 + inner
            base = pl.multiple_of(token * tiles, tiles)
            d = [d_s[pl.ds(base + 8 * p, 8), :] for p in range(packs)]
            u = [u_s[pl.ds(base + 8 * p, 8), :] for p in range(packs)]
            y = [None] * packs
            for n in range(STATE):
                b = bc_s[n, pl.ds(token, 1), :]
                c = bc_s[STATE + n, pl.ds(token, 1), :]
                for p in range(packs):
                    k = n * packs + p
                    fade = jnp.exp2(d[p] * rate_ref[n, 8 * p : 8 * p + 8, :])
                    states[k] = fade * states[k] + u[p] * b
                    term = c * states[k]
                    y[p] = term if y[p] is None else y[p] + term
            for p in range(packs):
                y_s[pl.ds(base + 8 * p, 8), :] = y[p]
        return tuple(states)

    start = tuple(
        h0_ref[n, 8 * p : 8 * p + 8, :] for n in range(STATE) for p in range(packs)
    )
    lax.fori_loop(0, rows // 8, advance, start)
    for tile in range(tiles):
        at = slice(tile * LANES, (tile + 1) * LANES)
        y = y_s[pl.ds(tile, rows, stride=tiles), :]
        z = z_ref[:, at].astype(jnp.float32)
        y = y + skip_ref[:, at] * x_ref[:, at].astype(jnp.float32)
        o_ref[:, at] = (y * (z / (1.0 + jnp.exp(-z)))).astype(o_ref.dtype)


def scan_layer(cols, dt_proj, dt_bias, mamba_x, gate_z, decay_rate, skip_gain, start_state):
    rows, width = mamba_x.shape
    tiles = width // LANES
    rate = (decay_rate * (-LOG2E)).reshape(STATE, tiles, LANES)
    start = start_state.astype(jnp.float32).reshape(STATE, tiles, LANES)
    return pl.pallas_call(
        scan_kernel,
        out_shape=jax.ShapeDtypeStruct((rows, width), jnp.bfloat16),
        in_specs=[pl.BlockSpec(memory_space=pltpu.VMEM)] * 8,
        out_specs=pl.BlockSpec(memory_space=pltpu.VMEM),
        scratch_shapes=[
            pltpu.VMEM((rows * tiles, LANES), jnp.float32),
            pltpu.VMEM((rows * tiles, LANES), jnp.float32),
            pltpu.VMEM((rows * tiles, LANES), jnp.float32),
            pltpu.VMEM((2 * STATE, rows, LANES), jnp.float32),
        ],
        compiler_params=pltpu.CompilerParams(vmem_limit_bytes=56 * 2**20),
        cost_estimate=pl.CostEstimate(
            flops=30 * 10**9, bytes_accessed=10 * 2**20, transcendentals=rows * STATE * width
        ),
        name="scan_tokens",
    )(cols, dt_proj, dt_bias[None], mamba_x, gate_z, rate, skip_gain[None], start)


def body(
    queries,
    suffix_kv,
    page_pool,
    prefix_pages,
    prefix_len,
    mamba_x,
    gate_z,
    x_proj,
    dt_proj,
    dt_bias,
    decay_rate,
    skip_gain,
    state_pool,
    state_src,
):
    devices = lax.axis_size("req")
    cap = max(3, MAXPG // devices + 1)
    pool_dev = page_pool.shape[0]
    spool = state_pool.shape[0]
    places = page_places(prefix_pages[0], pool_dev, cap)
    wanted = pack_asks(prefix_pages[0], places, pool_dev, jnp.arange(devices * cap)).reshape(
        devices, cap
    )
    my_src = state_src[0]
    state_want = jnp.where(jnp.arange(devices) == my_src // spool, my_src % spool, -1)[:, None]
    asks = lax.all_to_all(
        jnp.concatenate([wanted, state_want], axis=1), "req", split_axis=0, concat_axis=0, tiled=True
    )
    partial_cols = jnp.dot(mamba_x, x_proj, preferred_element_type=jnp.float32)
    cols = lax.psum(partial_cols.astype(jnp.bfloat16), "tp")
    state_asks = asks[:, cap]
    state_send = state_pool[jnp.where(state_asks >= 0, state_asks, 0)]
    got_states = lax.all_to_all(state_send, "req", split_axis=0, concat_axis=0, tiled=True)
    sends = gather_pages(page_pool, asks[:, :cap].reshape(-1))
    got = [lax.all_to_all(send, "req", split_axis=0, concat_axis=0, tiled=True) for send in sends]
    start_state = lax.dynamic_index_in_dim(got_states, my_src // spool, 0, keepdims=False)
    mamba_out = scan_layer(
        cols, dt_proj, dt_bias, mamba_x, gate_z, decay_rate, skip_gain, start_state
    )
    attn_out = None
    for part, pages in enumerate(got):
        attn_out = attend(part, places, prefix_len, queries, suffix_kv, pages, attn_out)
    return (attn_out, mamba_out)


def solution(mesh):
    return jax.shard_map(
        body,
        mesh=mesh,
        in_specs=(
            P("req", "tp"),
            P(None, "req", "tp"),
            P("req", None, None, "tp"),
            P("req", None),
            P("req"),
            P("req", "tp"),
            P("req", "tp"),
            P("tp", None),
            P(None, "tp"),
            P("tp"),
            P(None, "tp"),
            P("tp"),
            P("req", None, "tp"),
            P("req"),
        ),
        out_specs=(P("req", "tp"), P("req", "tp")),
        check_vma=False,
    )
```

```python
import functools
import math

import jax
import jax.numpy as jnp
from jax import lax
from jax.experimental import pallas as pl
from jax.experimental.pallas import tpu as pltpu
from jax.sharding import PartitionSpec as P

HEADS = 64
KV_HEADS = 8
HEAD_DIM = 128
STATE = 16
DT_RANK = 512
MAXPG = 64
LANES = 128
KEY_BLOCK = 1024
STEP_HEADS = 2
LOG2E = 1.4426950408889634


def page_places(pages, pool_dev, cap):
    keeper = jnp.where(pages >= 0, pages // pool_dev, -1)
    index = jnp.arange(pages.shape[-1])
    earlier = (keeper[..., :, None] == keeper[..., None, :]) & (index[None, :] < index[:, None])
    rank = jnp.sum(earlier.astype(jnp.int32), axis=-1)
    return jnp.where(pages >= 0, keeper * cap + rank, -1)


def pack_asks(pages, places, pool_dev, targets):
    local = jnp.where(pages >= 0, pages % pool_dev, 0)
    hit = places[..., None, :] == targets[:, None]
    return jnp.sum(jnp.where(hit, local[..., None, :] + 1, 0), axis=-1) - 1


def gather_kernel(part, asks, pool, out, held, sem):
    slots = held.shape[0]

    def start(slot, carry):
        page = jnp.maximum(asks[slot], 0)
        pltpu.make_async_copy(
            pool.at[page, :, :, pl.ds(part * LANES, LANES)], held.at[slot], sem.at[0]
        ).start()
        return carry

    lax.fori_loop(0, slots, start, 0)
    pltpu.make_async_copy(held, held, sem.at[0]).wait()
    whole = pltpu.make_async_copy(held, out, sem.at[1])
    whole.start()
    whole.wait()


def gather_pages(part, page_pool, asks):
    shape = asks.shape + page_pool.shape[1:3] + (LANES,)
    return pl.pallas_call(
        functools.partial(gather_kernel, part),
        out_shape=jax.ShapeDtypeStruct(shape, page_pool.dtype),
        in_specs=[
            pl.BlockSpec(memory_space=pltpu.SMEM),
            pl.BlockSpec(memory_space=pl.ANY),
        ],
        out_specs=pl.BlockSpec(memory_space=pl.ANY),
        scratch_shapes=[
            pltpu.VMEM(shape, page_pool.dtype),
            pltpu.SemaphoreType.DMA((2,)),
        ],
        compiler_params=pltpu.CompilerParams(vmem_limit_bytes=48 * 2**20),
        cost_estimate=pl.CostEstimate(flops=0, bytes_accessed=8 * 2**20, transcendentals=0),
        name="gather_pages",
    )(asks, page_pool)


def dot_nt(a, b):
    return lax.dot_general(a, b, (((1,), (1,)), ((), ())), preferred_element_type=jnp.float32)


def attend_kernel(places, plen_ref, q_ref, kv_ref, pages_ref, *rest):
    o_ref, k_s, v_s, sv_s, m_s, a_s, sem = rest[-7:]
    rows = q_ref.shape[0]
    page_rows = pages_ref.shape[2]
    keys = k_s.shape[0]
    slots = keys // page_rows
    scale = HEAD_DIM ** (-0.5) * LOG2E
    first = pl.program_id(0) == 0

    @pl.when(first)
    def _():
        def start(slot, carry):
            page = jnp.maximum(places[slot], 0)
            at = pl.ds(pl.multiple_of(slot * page_rows, page_rows), page_rows)
            pltpu.make_async_copy(pages_ref.at[page, 0], k_s.at[at], sem.at[0]).start()
            pltpu.make_async_copy(
                pages_ref.at[page, 1], v_s.at[at, pl.ds(0, LANES)], sem.at[1]
            ).start()
            return carry

        lax.fori_loop(0, slots, start, 0)
        v_s[:, LANES:] = jnp.ones((keys, LANES), v_s.dtype)
        sv_s[:, :LANES] = kv_ref[1]
        sv_s[:, LANES:] = jnp.ones((rows, LANES), sv_s.dtype)

    half = rows // 2
    for head in range(STEP_HEADS):
        for part in range(2):
            own = slice(part * half, (part + 1) * half)
            seen = (part + 1) * half
            q = q_ref[own, head * LANES : (head + 1) * LANES]
            s = dot_nt(q, kv_ref[0, :seen]) * scale
            row = lax.broadcasted_iota(jnp.int32, s.shape, 0) + part * half
            col = lax.broadcasted_iota(jnp.int32, s.shape, 1)
            s = jnp.where(col <= row, s, -1e30)
            m = jnp.max(s, axis=1, keepdims=True)
            p = jnp.exp2(s - m).astype(jnp.bfloat16)
            m_s[head, own] = jnp.broadcast_to(m, (half, LANES))
            a_s[head, own] = jnp.dot(p, sv_s[:seen], preferred_element_type=jnp.float32)

    @pl.when(first)
    def _():
        pltpu.make_async_copy(k_s, k_s, sem.at[0]).wait()
        pltpu.make_async_copy(v_s.at[:, pl.ds(0, LANES)], v_s.at[:, pl.ds(0, LANES)], sem.at[1]).wait()

    plen = plen_ref[0]
    last = (plen + KEY_BLOCK - 1) // KEY_BLOCK - 1

    def fold(block, masked):
        at = pl.ds(pl.multiple_of(block * KEY_BLOCK, KEY_BLOCK), KEY_BLOCK)
        k = k_s[at]
        v = v_s[at]
        if masked:
            col = lax.broadcasted_iota(jnp.int32, (1, KEY_BLOCK), 1) + block * KEY_BLOCK
            bias = jnp.where(col < plen, 0.0, -1e30)
        for head in range(STEP_HEADS):
            q = q_ref[:, head * LANES : (head + 1) * LANES]
            s = dot_nt(q, k) * scale
            if masked:
                s = s + bias
            old = m_s[head]
            new = jnp.maximum(old, jnp.max(s, axis=1, keepdims=True))
            m_s[head] = new
            fade = jnp.exp2(old - new)
            p = jnp.exp2(s - jnp.tile(new, (1, KEY_BLOCK // LANES))).astype(jnp.bfloat16)
            a_s[head] = a_s[head] * jnp.tile(fade, (1, 2)) + jnp.dot(
                p, v, preferred_element_type=jnp.float32
            )

    def visit(block, carry):
        fold(block, False)
        return carry

    lax.fori_loop(0, last, visit, 0)
    fold(last, True)
    for head in range(STEP_HEADS):
        o_ref[:, head * LANES : (head + 1) * LANES] = (
            a_s[head, :, :LANES] / a_s[head, :, LANES:]
        ).astype(o_ref.dtype)


def attend(part, places, plen, queries, suffix_kv, pages, out):
    rows, width = queries.shape
    group = HEADS // KV_HEADS
    steps = group // STEP_HEADS
    wide = STEP_HEADS * HEAD_DIM
    keys = places.shape[0] * pages.shape[2]
    in_specs = [
        pl.BlockSpec((rows, wide), lambda i, *_: (0, part * steps + i)),
        pl.BlockSpec((2, rows, HEAD_DIM), lambda i, *_: (0, 0, part)),
        pl.BlockSpec(memory_space=pl.ANY),
    ]
    args = [places, plen, queries, suffix_kv, pages]
    aliases = {}
    if out is not None:
        in_specs.append(pl.BlockSpec(memory_space=pl.ANY))
        args.append(out)
        aliases = {5: 0}
    flops = 4 * rows * group * (keys + rows) * HEAD_DIM
    return pl.pallas_call(
        attend_kernel,
        out_shape=jax.ShapeDtypeStruct((rows, width), jnp.bfloat16),
        grid_spec=pltpu.PrefetchScalarGridSpec(
            num_scalar_prefetch=2,
            grid=(steps,),
            in_specs=in_specs,
            out_specs=pl.BlockSpec((rows, wide), lambda i, *_: (0, part * steps + i)),
            scratch_shapes=[
                pltpu.VMEM((keys, HEAD_DIM), jnp.bfloat16),
                pltpu.VMEM((keys, 2 * LANES), jnp.bfloat16),
                pltpu.VMEM((rows, 2 * LANES), jnp.bfloat16),
                pltpu.VMEM((STEP_HEADS, rows, LANES), jnp.float32),
                pltpu.VMEM((STEP_HEADS, rows, 2 * LANES), jnp.float32),
                pltpu.SemaphoreType.DMA((2,)),
            ],
        ),
        input_output_aliases=aliases,
        compiler_params=pltpu.CompilerParams(vmem_limit_bytes=48 * 2**20),
        cost_estimate=pl.CostEstimate(
            flops=2 * flops, bytes_accessed=8 * 2**20, transcendentals=flops // (4 * HEAD_DIM)
        ),
        name="attend_cached",
    )(*args)


def scan_kernel(
    cols_ref, dtp_ref, bias_ref, x_ref, z_ref, rate_ref, skip_ref, h0_ref, o_ref, d_s, u_s, y_s, bc_s
):
    rows, width = x_ref.shape
    tiles = width // LANES
    packs = tiles // 8
    low = cols_ref[:, :DT_RANK].astype(jnp.float32)
    low = (low * lax.rsqrt(jnp.mean(low * low, axis=-1, keepdims=True) + 1e-06)).astype(
        jnp.bfloat16
    )
    for tile in range(tiles):
        at = slice(tile * LANES, (tile + 1) * LANES)
        if tile % 2 == 0:
            two = slice(tile * LANES, (tile + 2) * LANES)
            pair = (
                jnp.dot(low, dtp_ref[:, two], preferred_element_type=jnp.float32)
                + bias_ref[:, two]
            )
        v = pair[:, (tile % 2) * LANES : (tile % 2 + 1) * LANES]
        step = jnp.maximum(v, 0.0) + jnp.log1p(jnp.exp(-jnp.abs(v)))
        spread = pl.ds(tile, rows, stride=tiles)
        d_s[spread, :] = step
        u_s[spread, :] = step * x_ref[:, at].astype(jnp.float32)
    maps = cols_ref[:, DT_RANK:].astype(jnp.float32)
    for entry in range(2 * STATE):
        bc_s[entry] = jnp.broadcast_to(maps[:, entry : entry + 1], (rows, LANES))

    def advance(group, states):
        states = list(states)
        for inner in range(8):
            token = group * 8 + inner
            base = pl.multiple_of(token * tiles, tiles)
            d = [d_s[pl.ds(base + 8 * p, 8), :] for p in range(packs)]
            u = [u_s[pl.ds(base + 8 * p, 8), :] for p in range(packs)]
            y = [None] * packs
            for n in range(STATE):
                b = bc_s[n, pl.ds(token, 1), :]
                c = bc_s[STATE + n, pl.ds(token, 1), :]
                for p in range(packs):
                    k = n * packs + p
                    fade = jnp.exp2(d[p] * rate_ref[n, 8 * p : 8 * p + 8, :])
                    states[k] = fade * states[k] + u[p] * b
                    term = c * states[k]
                    y[p] = term if y[p] is None else y[p] + term
            for p in range(packs):
                y_s[pl.ds(base + 8 * p, 8), :] = y[p]
        return tuple(states)

    start = tuple(
        h0_ref[n, 8 * p : 8 * p + 8, :] for n in range(STATE) for p in range(packs)
    )
    lax.fori_loop(0, rows // 8, advance, start)
    for tile in range(tiles):
        at = slice(tile * LANES, (tile + 1) * LANES)
        y = y_s[pl.ds(tile, rows, stride=tiles), :]
        z = z_ref[:, at].astype(jnp.float32)
        y = y + skip_ref[:, at] * x_ref[:, at].astype(jnp.float32)
        o_ref[:, at] = (y * (z / (1.0 + jnp.exp(-z)))).astype(o_ref.dtype)


def scan_layer(cols, dt_proj, dt_bias, mamba_x, gate_z, decay_rate, skip_gain, start_state):
    rows, width = mamba_x.shape
    tiles = width // LANES
    rate = (decay_rate * (-LOG2E)).reshape(STATE, tiles, LANES)
    start = start_state.astype(jnp.float32).reshape(STATE, tiles, LANES)
    return pl.pallas_call(
        scan_kernel,
        out_shape=jax.ShapeDtypeStruct((rows, width), jnp.bfloat16),
        in_specs=[pl.BlockSpec(memory_space=pltpu.VMEM)] * 8,
        out_specs=pl.BlockSpec(memory_space=pltpu.VMEM),
        scratch_shapes=[
            pltpu.VMEM((rows * tiles, LANES), jnp.float32),
            pltpu.VMEM((rows * tiles, LANES), jnp.float32),
            pltpu.VMEM((rows * tiles, LANES), jnp.float32),
            pltpu.VMEM((2 * STATE, rows, LANES), jnp.float32),
        ],
        compiler_params=pltpu.CompilerParams(vmem_limit_bytes=56 * 2**20),
        cost_estimate=pl.CostEstimate(
            flops=30 * 10**9, bytes_accessed=10 * 2**20, transcendentals=rows * STATE * width
        ),
        name="scan_tokens",
    )(cols, dt_proj, dt_bias[None], mamba_x, gate_z, rate, skip_gain[None], start)


def body(
    queries,
    suffix_kv,
    page_pool,
    prefix_pages,
    prefix_len,
    mamba_x,
    gate_z,
    x_proj,
    dt_proj,
    dt_bias,
    decay_rate,
    skip_gain,
    state_pool,
    state_src,
):
    devices = lax.axis_size("req")
    cap = max(3, MAXPG // devices + 1)
    pool_dev = page_pool.shape[0]
    spool = state_pool.shape[0]
    places = page_places(prefix_pages[0], pool_dev, cap)
    wanted = pack_asks(prefix_pages[0], places, pool_dev, jnp.arange(devices * cap)).reshape(
        devices, cap
    )
    my_src = state_src[0]
    state_want = jnp.where(jnp.arange(devices) == my_src // spool, my_src % spool, -1)[:, None]
    wanted = jnp.concatenate([wanted, state_want], axis=1)
    partial_cols = jnp.dot(mamba_x, x_proj, preferred_element_type=jnp.float32)
    partial_cols, wanted = lax.optimization_barrier((partial_cols.astype(jnp.bfloat16), wanted))
    cols = lax.psum(partial_cols, "tp")
    asks = lax.all_to_all(wanted, "req", split_axis=0, concat_axis=0, tiled=True)
    page_asks = asks[:, :cap].reshape(-1)
    state_asks = asks[:, cap]
    state_send = state_pool[jnp.where(state_asks >= 0, state_asks, 0)]
    got_states = lax.all_to_all(state_send, "req", split_axis=0, concat_axis=0, tiled=True)
    start_state = lax.dynamic_index_in_dim(got_states, my_src // spool, 0, keepdims=False)
    parts = page_pool.shape[3] // LANES
    attn_out = mamba_out = None
    for part in range(parts):
        send = gather_pages(part, page_pool, page_asks)
        if part == 1:
            send, mamba_out = lax.optimization_barrier((send, mamba_out))
        pages = lax.all_to_all(send, "req", split_axis=0, concat_axis=0, tiled=True)
        if part == 0:
            mamba_out = scan_layer(
                cols, dt_proj, dt_bias, mamba_x, gate_z, decay_rate, skip_gain, start_state
            )
        attn_out = attend(part, places, prefix_len, queries, suffix_kv, pages, attn_out)
    return (attn_out, mamba_out)


def solution(mesh):
    return jax.shard_map(
        body,
        mesh=mesh,
        in_specs=(
            P("req", "tp"),
            P(None, "req", "tp"),
            P("req", None, None, "tp"),
            P("req", None),
            P("req"),
            P("req", "tp"),
            P("req", "tp"),
            P("tp", None),
            P(None, "tp"),
            P("tp"),
            P(None, "tp"),
            P("tp"),
            P("req", None, "tp"),
            P("req"),
        ),
        out_specs=(P("req", "tp"), P("req", "tp")),
        check_vma=False,
    )
```

```python
import functools
import math

import jax
import jax.numpy as jnp
from jax import lax
from jax.experimental import pallas as pl
from jax.experimental.pallas import tpu as pltpu
from jax.sharding import PartitionSpec as P

HEADS = 64
KV_HEADS = 8
HEAD_DIM = 128
STATE = 16
DT_RANK = 512
MAXPG = 64
LANES = 128
KEY_BLOCK = 1024
STEP_HEADS = 2
LOG2E = 1.4426950408889634


def page_places(pages, pool_dev, cap):
    keeper = jnp.where(pages >= 0, pages // pool_dev, -1)
    index = jnp.arange(pages.shape[-1])
    earlier = (keeper[..., :, None] == keeper[..., None, :]) & (index[None, :] < index[:, None])
    rank = jnp.sum(earlier.astype(jnp.int32), axis=-1)
    return jnp.where(pages >= 0, keeper * cap + rank, -1)


def pack_asks(pages, places, pool_dev, targets):
    local = jnp.where(pages >= 0, pages % pool_dev, 0)
    hit = places[..., None, :] == targets[:, None]
    return jnp.sum(jnp.where(hit, local[..., None, :] + 1, 0), axis=-1) - 1


def gather_kernel(part, asks, pool, out, held, sem):
    slots = held.shape[0]

    def start(slot, carry):
        page = jnp.maximum(asks[slot], 0)
        pltpu.make_async_copy(
            pool.at[page, :, :, pl.ds(part * LANES, LANES)], held.at[slot], sem.at[0]
        ).start()
        return carry

    lax.fori_loop(0, slots, start, 0)
    pltpu.make_async_copy(held, held, sem.at[0]).wait()
    whole = pltpu.make_async_copy(held, out, sem.at[1])
    whole.start()
    whole.wait()


def gather_pages(part, page_pool, asks):
    shape = asks.shape + page_pool.shape[1:3] + (LANES,)
    return pl.pallas_call(
        functools.partial(gather_kernel, part),
        out_shape=jax.ShapeDtypeStruct(shape, page_pool.dtype),
        in_specs=[
            pl.BlockSpec(memory_space=pltpu.SMEM),
            pl.BlockSpec(memory_space=pl.ANY),
        ],
        out_specs=pl.BlockSpec(memory_space=pl.ANY),
        scratch_shapes=[
            pltpu.VMEM(shape, page_pool.dtype),
            pltpu.SemaphoreType.DMA((2,)),
        ],
        compiler_params=pltpu.CompilerParams(vmem_limit_bytes=48 * 2**20),
        cost_estimate=pl.CostEstimate(flops=0, bytes_accessed=8 * 2**20, transcendentals=0),
        name="gather_pages",
    )(asks, page_pool)


def dot_nt(a, b):
    return lax.dot_general(a, b, (((1,), (1,)), ((), ())), preferred_element_type=jnp.float32)


def attend_kernel(places, plen_ref, q_ref, kv_ref, pages_ref, *rest):
    o_ref, k_s, v_s, sv_s, m_s, a_s, sem = rest[-7:]
    rows = q_ref.shape[0]
    page_rows = pages_ref.shape[2]
    keys = k_s.shape[0]
    slots = keys // page_rows
    scale = HEAD_DIM ** (-0.5) * LOG2E
    first = pl.program_id(0) == 0

    @pl.when(first)
    def _():
        def start(slot, carry):
            page = jnp.maximum(places[slot], 0)
            at = pl.ds(pl.multiple_of(slot * page_rows, page_rows), page_rows)
            pltpu.make_async_copy(pages_ref.at[page, 0], k_s.at[at], sem.at[0]).start()
            pltpu.make_async_copy(
                pages_ref.at[page, 1], v_s.at[at, pl.ds(0, LANES)], sem.at[1]
            ).start()
            return carry

        lax.fori_loop(0, slots, start, 0)
        v_s[:, LANES:] = jnp.ones((keys, LANES), v_s.dtype)
        sv_s[:, :LANES] = kv_ref[1]
        sv_s[:, LANES:] = jnp.ones((rows, LANES), sv_s.dtype)

    half = rows // 2
    for head in range(STEP_HEADS):
        for part in range(2):
            own = slice(part * half, (part + 1) * half)
            seen = (part + 1) * half
            q = q_ref[own, head * LANES : (head + 1) * LANES]
            s = dot_nt(q, kv_ref[0, :seen]) * scale
            row = lax.broadcasted_iota(jnp.int32, s.shape, 0) + part * half
            col = lax.broadcasted_iota(jnp.int32, s.shape, 1)
            s = jnp.where(col <= row, s, -1e30)
            m = jnp.max(s, axis=1, keepdims=True)
            p = jnp.exp2(s - m).astype(jnp.bfloat16)
            m_s[head, own] = jnp.broadcast_to(m, (half, LANES))
            a_s[head, own] = jnp.dot(p, sv_s[:seen], preferred_element_type=jnp.float32)

    @pl.when(first)
    def _():
        pltpu.make_async_copy(k_s, k_s, sem.at[0]).wait()
        pltpu.make_async_copy(v_s.at[:, pl.ds(0, LANES)], v_s.at[:, pl.ds(0, LANES)], sem.at[1]).wait()

    plen = plen_ref[0]
    last = (plen + KEY_BLOCK - 1) // KEY_BLOCK - 1

    def fold(block, masked):
        at = pl.ds(pl.multiple_of(block * KEY_BLOCK, KEY_BLOCK), KEY_BLOCK)
        k = k_s[at]
        v = v_s[at]
        if masked:
            col = lax.broadcasted_iota(jnp.int32, (1, KEY_BLOCK), 1) + block * KEY_BLOCK
            bias = jnp.where(col < plen, 0.0, -1e30)
        for head in range(STEP_HEADS):
            q = q_ref[:, head * LANES : (head + 1) * LANES]
            s = dot_nt(q, k) * scale
            if masked:
                s = s + bias
            old = m_s[head]
            new = jnp.maximum(old, jnp.max(s, axis=1, keepdims=True))
            m_s[head] = new
            fade = jnp.exp2(old - new)
            p = jnp.exp2(s - jnp.tile(new, (1, KEY_BLOCK // LANES))).astype(jnp.bfloat16)
            a_s[head] = a_s[head] * jnp.tile(fade, (1, 2)) + jnp.dot(
                p, v, preferred_element_type=jnp.float32
            )

    def visit(block, carry):
        fold(block, False)
        return carry

    lax.fori_loop(0, last, visit, 0)
    fold(last, True)
    for head in range(STEP_HEADS):
        o_ref[:, head * LANES : (head + 1) * LANES] = (
            a_s[head, :, :LANES] / a_s[head, :, LANES:]
        ).astype(o_ref.dtype)


def attend(part, places, plen, queries, suffix_kv, pages, out):
    rows, width = queries.shape
    group = HEADS // KV_HEADS
    steps = group // STEP_HEADS
    wide = STEP_HEADS * HEAD_DIM
    keys = places.shape[0] * pages.shape[2]
    in_specs = [
        pl.BlockSpec((rows, wide), lambda i, *_: (0, part * steps + i)),
        pl.BlockSpec((2, rows, HEAD_DIM), lambda i, *_: (0, 0, part)),
        pl.BlockSpec(memory_space=pl.ANY),
    ]
    args = [places, plen, queries, suffix_kv, pages]
    aliases = {}
    if out is not None:
        in_specs.append(pl.BlockSpec(memory_space=pl.ANY))
        args.append(out)
        aliases = {5: 0}
    flops = 4 * rows * group * (keys + rows) * HEAD_DIM
    return pl.pallas_call(
        attend_kernel,
        out_shape=jax.ShapeDtypeStruct((rows, width), jnp.bfloat16),
        grid_spec=pltpu.PrefetchScalarGridSpec(
            num_scalar_prefetch=2,
            grid=(steps,),
            in_specs=in_specs,
            out_specs=pl.BlockSpec((rows, wide), lambda i, *_: (0, part * steps + i)),
            scratch_shapes=[
                pltpu.VMEM((keys, HEAD_DIM), jnp.bfloat16),
                pltpu.VMEM((keys, 2 * LANES), jnp.bfloat16),
                pltpu.VMEM((rows, 2 * LANES), jnp.bfloat16),
                pltpu.VMEM((STEP_HEADS, rows, LANES), jnp.float32),
                pltpu.VMEM((STEP_HEADS, rows, 2 * LANES), jnp.float32),
                pltpu.SemaphoreType.DMA((2,)),
            ],
        ),
        input_output_aliases=aliases,
        compiler_params=pltpu.CompilerParams(vmem_limit_bytes=48 * 2**20),
        cost_estimate=pl.CostEstimate(
            flops=2 * flops, bytes_accessed=8 * 2**20, transcendentals=flops // (4 * HEAD_DIM)
        ),
        name="attend_cached",
    )(*args)


def scan_kernel(
    cols_ref, dtp_ref, bias_ref, x_ref, z_ref, rate_ref, skip_ref, h0_ref, o_ref, d_s, u_s, y_s, bc_s
):
    rows, width = x_ref.shape
    tiles = width // LANES
    packs = tiles // 8
    low = cols_ref[:, :DT_RANK].astype(jnp.float32)
    low = (low * lax.rsqrt(jnp.mean(low * low, axis=-1, keepdims=True) + 1e-06)).astype(
        jnp.bfloat16
    )
    for tile in range(tiles):
        at = slice(tile * LANES, (tile + 1) * LANES)
        if tile % 2 == 0:
            two = slice(tile * LANES, (tile + 2) * LANES)
            pair = (
                jnp.dot(low, dtp_ref[:, two], preferred_element_type=jnp.float32)
                + bias_ref[:, two]
            )
        v = pair[:, (tile % 2) * LANES : (tile % 2 + 1) * LANES]
        step = jnp.maximum(v, 0.0) + jnp.log1p(jnp.exp(-jnp.abs(v)))
        spread = pl.ds(tile, rows, stride=tiles)
        d_s[spread, :] = step
        u_s[spread, :] = step * x_ref[:, at].astype(jnp.float32)
    maps = cols_ref[:, DT_RANK:].astype(jnp.float32)
    for entry in range(2 * STATE):
        bc_s[entry] = jnp.broadcast_to(maps[:, entry : entry + 1], (rows, LANES))

    def advance(group, states):
        states = list(states)
        for inner in range(8):
            token = group * 8 + inner
            base = pl.multiple_of(token * tiles, tiles)
            d = [d_s[pl.ds(base + 8 * p, 8), :] for p in range(packs)]
            u = [u_s[pl.ds(base + 8 * p, 8), :] for p in range(packs)]
            y = [None] * packs
            for n in range(STATE):
                b = bc_s[n, pl.ds(token, 1), :]
                c = bc_s[STATE + n, pl.ds(token, 1), :]
                for p in range(packs):
                    k = n * packs + p
                    fade = jnp.exp2(d[p] * rate_ref[n, 8 * p : 8 * p + 8, :])
                    states[k] = fade * states[k] + u[p] * b
                    term = c * states[k]
                    y[p] = term if y[p] is None else y[p] + term
            for p in range(packs):
                y_s[pl.ds(base + 8 * p, 8), :] = y[p]
        return tuple(states)

    start = tuple(
        h0_ref[n, 8 * p : 8 * p + 8, :] for n in range(STATE) for p in range(packs)
    )
    lax.fori_loop(0, rows // 8, advance, start)
    for tile in range(tiles):
        at = slice(tile * LANES, (tile + 1) * LANES)
        y = y_s[pl.ds(tile, rows, stride=tiles), :]
        z = z_ref[:, at].astype(jnp.float32)
        y = y + skip_ref[:, at] * x_ref[:, at].astype(jnp.float32)
        o_ref[:, at] = (y * (z / (1.0 + jnp.exp(-z)))).astype(o_ref.dtype)


def scan_layer(cols, dt_proj, dt_bias, mamba_x, gate_z, decay_rate, skip_gain, start_state):
    rows, width = mamba_x.shape
    tiles = width // LANES
    rate = (decay_rate * (-LOG2E)).reshape(STATE, tiles, LANES)
    start = start_state.astype(jnp.float32).reshape(STATE, tiles, LANES)
    return pl.pallas_call(
        scan_kernel,
        out_shape=jax.ShapeDtypeStruct((rows, width), jnp.bfloat16),
        in_specs=[pl.BlockSpec(memory_space=pltpu.VMEM)] * 8,
        out_specs=pl.BlockSpec(memory_space=pltpu.VMEM),
        scratch_shapes=[
            pltpu.VMEM((rows * tiles, LANES), jnp.float32),
            pltpu.VMEM((rows * tiles, LANES), jnp.float32),
            pltpu.VMEM((rows * tiles, LANES), jnp.float32),
            pltpu.VMEM((2 * STATE, rows, LANES), jnp.float32),
        ],
        compiler_params=pltpu.CompilerParams(vmem_limit_bytes=56 * 2**20),
        cost_estimate=pl.CostEstimate(
            flops=30 * 10**9, bytes_accessed=10 * 2**20, transcendentals=rows * STATE * width
        ),
        name="scan_tokens",
    )(cols, dt_proj, dt_bias[None], mamba_x, gate_z, rate, skip_gain[None], start)


def body(
    queries,
    suffix_kv,
    page_pool,
    prefix_pages,
    prefix_len,
    mamba_x,
    gate_z,
    x_proj,
    dt_proj,
    dt_bias,
    decay_rate,
    skip_gain,
    state_pool,
    state_src,
):
    devices = lax.axis_size("req")
    cap = max(3, MAXPG // devices + 1)
    pool_dev = page_pool.shape[0]
    spool = state_pool.shape[0]
    places = page_places(prefix_pages[0], pool_dev, cap)
    wanted = pack_asks(prefix_pages[0], places, pool_dev, jnp.arange(devices * cap)).reshape(
        devices, cap
    )
    my_src = state_src[0]
    state_want = jnp.where(jnp.arange(devices) == my_src // spool, my_src % spool, -1)[:, None]
    wanted = jnp.concatenate([wanted, state_want], axis=1)
    partial_cols = jnp.dot(mamba_x, x_proj, preferred_element_type=jnp.float32)
    partial_cols, wanted = lax.optimization_barrier((partial_cols.astype(jnp.bfloat16), wanted))
    cols = lax.psum(partial_cols, "tp")
    asks = lax.all_to_all(wanted, "req", split_axis=0, concat_axis=0, tiled=True)
    page_asks = asks[:, :cap].reshape(-1)
    state_asks = asks[:, cap]
    state_send = state_pool[jnp.where(state_asks >= 0, state_asks, 0)]
    got_states = lax.all_to_all(state_send, "req", split_axis=0, concat_axis=0, tiled=True)
    start_state = lax.dynamic_index_in_dim(got_states, my_src // spool, 0, keepdims=False)
    parts = page_pool.shape[3] // LANES
    attn_out = mamba_out = None
    for part in range(parts):
        send = gather_pages(part, page_pool, page_asks)
        if part == 0:
            send, cols = lax.optimization_barrier((send, cols))
        if part == 1:
            send, mamba_out = lax.optimization_barrier((send, mamba_out))
        pages = lax.all_to_all(send, "req", split_axis=0, concat_axis=0, tiled=True)
        if part == 0:
            mamba_out = scan_layer(
                cols, dt_proj, dt_bias, mamba_x, gate_z, decay_rate, skip_gain, start_state
            )
        attn_out = attend(part, places, prefix_len, queries, suffix_kv, pages, attn_out)
    return (attn_out, mamba_out)


def solution(mesh):
    return jax.shard_map(
        body,
        mesh=mesh,
        in_specs=(
            P("req", "tp"),
            P(None, "req", "tp"),
            P("req", None, None, "tp"),
            P("req", None),
            P("req"),
            P("req", "tp"),
            P("req", "tp"),
            P("tp", None),
            P(None, "tp"),
            P("tp"),
            P(None, "tp"),
            P("tp"),
            P("req", None, "tp"),
            P("req"),
        ),
        out_specs=(P("req", "tp"), P("req", "tp")),
        check_vma=False,
    )
```
